32 devices in a mesh: dp: 4 (over x, core), expert: 2 (over y), tp: 4 (over z).
Axes of the slice: x: 2, y: 2, z: 4, core: 2. Of those that a mesh axis runs over, the one named last changes fastest.
Arguments:
- hidden: bfloat16 [16, 8, 96, 5632], P('expert', 'dp', None, 'tp'), parts along dimension 1, may hold values from -6 to 6
- down_weight: bfloat16 [16, 5632, 3072], P('expert', 'tp'), may hold values from -0.078125 to 0.078125
- routes: int32 [2048, 4], P(('dp', 'expert')), parts along dimension 0, may hold values from 0 to 15, all different within a row; in each aligned block of 256 rows (0 to 255, 256 to 511, ...) at most 96 rows name the same one
- route_weight: float32 [2048, 4], P(('dp', 'expert')), parts along dimension 0, may hold values from 0.05 to 1
- residual: bfloat16 [2048, 3072], P(('dp', 'expert'), 'tp'), parts along dimension 0, may hold values from -6 to 6
Outputs:
- mixed: bfloat16 [2048, 3072], P(('dp', 'expert'), 'tp'), parts along dimension 0
The draws below stay inside these ranges and needn't reach their ends.
There are 4 independent parts, one for each index of `dp`. The reference program is written for one: setup_inputs(seed, part) draws one part's arguments, and reference() takes and returns one part's arrays. A program takes and returns all parts, laid end to end along the dimension named above; an argument that names none is the same for every part. Nothing has to cross between parts.
Inputs may be any that keep to these rules, and one draw needn't show every extreme that they name: `routes`: each row names 4 different experts. Among the 256 rows of one source group no expert is named by more than 96 rows, a bound that some of them reach.
All inputs are finite; a program needn't handle non-finite values.
Results may differ from the reference program's by a relative error of at most 0.0095.
Values may be sent and summed in bfloat16 or wider, within the bound.
No kernel may reach another device: no remote copies, remote signals or barrier semaphores. Data moves between devices by JAX's collectives and lax.ppermute only.
A program may use at most 128 MiB of HBM per device.

```python
import math
import jax
import jax.numpy as jnp
import numpy as np
from jax import lax

D = 3072
FF = 5632
EXPERTS = 16
TOP = 4
TOK_DEV = 256
CAP = 96
SOURCES = 2
GROUPS = 4
HID_DEV = 1408
TOKENS = 512


def shard_levels(stream_key, shape, split, smallest, high):
    level, own = 1.0, jax.random.fold_in(stream_key, 6)
    for dim, shards_of in split:
        heights = jnp.exp(jax.random.uniform(jax.random.fold_in(own, dim), (shards_of,), jnp.float32, smallest / len(split), high / len(split)))
        level = level * jnp.repeat(heights, shape[dim] // shards_of).reshape([-1 if axis == dim else 1 for axis in range(len(shape))])
    return level


def deal_out(stream_key, own, number, rows, amount, top, limit, lean):
    ranking = jax.random.permutation(stream_key, amount)
    crowded, ordinary = shares(amount, rows * top, limit, lean, True), shares(amount, rows * top, limit, lean, False)
    places = jnp.arange(amount)

    def named(tallies, turn):
        used = int((tallies > 0).sum())
        fixed = max(1, used // 4)
        moved = fixed + (places - fixed + turn * (used - fixed)) % max(1, amount - fixed)
        return jnp.zeros((amount,), jnp.int32).at[ranking[jnp.where(places < fixed, places, moved)]].set(jnp.asarray(tallies, jnp.int32))

    tallies = jnp.where(number % 4 == 0, named(crowded, number // 4), named(ordinary, number - number // 4 - 1))
    mixed = jax.random.permutation(jax.random.fold_in(own, 3), amount)
    giver, taker = mixed[0:amount // 2 * 2:2], mixed[1:amount // 2 * 2:2]
    slack = jnp.minimum(tallies[giver] - 1, limit - tallies[taker]) // 2
    slack = jnp.where((giver == ranking[0]) | (taker == ranking[0]) | (tallies[taker] == 0), 0, jnp.maximum(slack, 0))
    moved = jax.random.randint(jax.random.fold_in(own, 4), (amount // 2,), 0, 1 << 20) % (slack + 1)
    tallies = tallies.at[giver].add(-moved).at[taker].add(moved)
    members = jnp.searchsorted(jnp.cumsum(tallies), jnp.arange(rows * top), side="right").astype(jnp.int32)
    table = members.reshape(top, rows).T
    table = table[jax.random.permutation(jax.random.fold_in(own, 1), rows)]
    turn = jax.random.randint(jax.random.fold_in(own, 2), (rows, 1), 0, top)
    return jnp.take_along_axis(table, (jnp.arange(top)[None, :] + turn) % top, axis=1)


def shares(count, total, bound, lean, full):
    weights = [(1 << 20) // math.isqrt(standing ** lean) + 1 for standing in range(1, count + 1)]
    largest = bound if full else min(bound, max(-(-total // count), total * weights[0] // sum(weights)))
    least = 1 if total - largest >= count - 1 else 0
    counts, surplus = [largest] + [least] * (count - 1), total - largest - least * (count - 1)
    while surplus > 0:
        free = [i for i in range(1, count) if counts[i] < largest] or [i for i in range(1, count) if counts[i] < bound]
        mass, budget = sum([weights[i] for i in free]), surplus
        for i in free:
            extra = min(bound - counts[i], max(1, budget * weights[i] // mass), surplus)
            counts[i] = counts[i] + extra
            surplus = surplus - extra
    return np.array(counts)


def scatter_about(key, shape, width, limit, split=(), held_as=jnp.bfloat16):
    entries = jax.random.normal(key, shape, jnp.float32) * width
    if len(split) > 0:
        entries = shard_levels(key, shape, split, -0.22, 0.18) * entries
    return jnp.clip(entries, min=-limit, max=limit).astype(held_as)


def setup_inputs(seed: int = 0, part: int = 0) -> dict:
    key_list = jax.random.split(jax.random.key(seed), 6)
    own_keys = jax.random.split(jax.random.fold_in(key_list[5], part), 6)
    hidden = scatter_about(own_keys[0], (EXPERTS, SOURCES, CAP, FF), 1.0, 6.0, ((0, 2), (3, 4)))
    down_weight = scatter_about(key_list[1], (EXPERTS, FF, D), FF ** -0.5, 0.078125, ((0, 2), (1, 4)))
    routes_keys = jax.random.split(jax.random.fold_in(own_keys[2], 1), TOKENS // TOK_DEV)
    routes_turns = jax.random.permutation(jax.random.fold_in(own_keys[2], 3), TOKENS // TOK_DEV)
    routes = jax.vmap(lambda own, number: deal_out(jax.random.fold_in(own_keys[2], 2), own, number, TOK_DEV, EXPERTS, TOP, CAP, 2))(routes_keys, routes_turns).reshape((TOKENS, TOP))
    route_weight = jnp.clip(jnp.exp(math.log(1.0) - 2.9957323 * jax.random.uniform(own_keys[3], (TOKENS, TOP), jnp.float32) ** shard_levels(own_keys[3], (TOKENS, TOP), ((0, 2),), -0.2, 0.2)), 0.05, 1.0)
    residual = scatter_about(own_keys[4], (TOKENS, D), 1.0, 6.0, ((0, 2), (1, 4)))
    return {"hidden": hidden, "down_weight": down_weight, "routes": routes, "route_weight": route_weight, "residual": residual}


def one_expert(operands):
    block_hidden, block_weight = operands
    hidden_groups = block_hidden.reshape(SOURCES * CAP, GROUPS, HID_DEV)
    weight_groups = block_weight.reshape(GROUPS, HID_DEV, D)
    running = jnp.zeros((SOURCES * CAP, D), jnp.float32)
    for group in range(GROUPS):
        partial_value = jnp.dot(hidden_groups[:, group, :], weight_groups[group], preferred_element_type=jnp.float32).astype(jnp.bfloat16)
        partial_value = lax.optimization_barrier(partial_value)
        running = running + partial_value.astype(jnp.float32)
    return running.reshape(SOURCES, CAP, D)


def reference(hidden, down_weight, routes, route_weight, residual):
    expert_out = lax.map(one_expert, (hidden, down_weight))
    grouped = routes.reshape(SOURCES, TOK_DEV, TOP)
    expert_ids = jnp.arange(EXPERTS, dtype=jnp.int32)
    onehot = jnp.sum((grouped[:, :, :, None] == expert_ids[None, None, None, :]).astype(jnp.int32), axis=2)
    before = jnp.cumsum(onehot, axis=1) - onehot
    slot_of = jnp.take_along_axis(before, grouped, axis=2).astype(jnp.int32)
    source_index = jnp.arange(SOURCES, dtype=jnp.int32)[:, None, None]
    picked = expert_out[grouped, source_index, slot_of]
    weights = route_weight.reshape(SOURCES, TOK_DEV, TOP)
    share = weights / jnp.sum(weights, axis=2, keepdims=True)
    expert_mix = jnp.sum(share[:, :, :, None] * picked, axis=2).reshape(TOKENS, D)
    return (residual.astype(jnp.float32) + expert_mix).astype(jnp.bfloat16)
```

```python
import functools

import jax
import jax.numpy as jnp
from jax import lax
from jax.experimental import pallas as pl
from jax.experimental.pallas import tpu as pltpu
from jax.sharding import PartitionSpec as P

LANES = 128
AHEAD = 2
BLOCKS = (3, 1, 2, 0)

VMEM = pl.BlockSpec(memory_space=pltpu.VMEM)
SMEM = pl.BlockSpec(memory_space=pltpu.SMEM)
ANY = pl.BlockSpec(memory_space=pl.ANY)


def table_kernel(capacity, ids_ref, routes_ref, weight_ref, table_ref):
    sources, tokens, width = table_ref.shape
    top = routes_ref.shape[2]
    local = width // capacity
    first = ids_ref[0] * local
    rows = lax.broadcasted_iota(jnp.int32, (tokens, tokens), 0)
    cols = lax.broadcasted_iota(jnp.int32, (tokens, tokens), 1)
    earlier = (cols < rows).astype(jnp.float32).astype(jnp.bfloat16)
    lanes = lax.broadcasted_iota(jnp.int32, (tokens, LANES), 1)
    places = lax.broadcasted_iota(jnp.int32, (tokens, width), 1)
    for source in range(sources):
        routes = routes_ref[source]
        weight = weight_ref[source]
        share = weight / jnp.sum(weight, axis=1, keepdims=True)
        matches = [(routes[:, k : k + 1] == lanes).astype(jnp.float32) for k in range(top)]
        onehot = functools.reduce(jnp.add, matches)
        before = jnp.dot(earlier, onehot.astype(jnp.bfloat16), preferred_element_type=jnp.float32)
        entry = jnp.zeros((tokens, width), jnp.float32)
        for k in range(top):
            slot = jnp.sum(matches[k] * before, axis=1, keepdims=True).astype(jnp.int32)
            expert = routes[:, k : k + 1] - first
            at = jnp.where((expert >= 0) & (expert < local), expert * capacity + slot, -1)
            entry = entry + jnp.where(places == at, share[:, k : k + 1], 0.0)
        table_ref[source] = entry.astype(table_ref.dtype)


def share_tables(ids, routes, weight, local, capacity):
    sources, tokens = routes.shape[:2]
    return pl.pallas_call(
        functools.partial(table_kernel, capacity),
        in_specs=[SMEM, VMEM, VMEM],
        out_specs=VMEM,
        out_shape=jax.ShapeDtypeStruct((sources, tokens, local * capacity), jnp.bfloat16),
        compiler_params=pltpu.CompilerParams(vmem_limit_bytes=16 << 20),
        name="tables",
    )(ids, routes, weight)


def chunk_kernel(chunk, chunks, pair, *refs):
    first, last = chunk == 0, chunk == chunks - 1
    refs = list(refs)
    ids_ref, hidden_ref, weight_ref, table_ref = refs[:4]
    del refs[:4]
    held_ref = None if first else refs.pop(0)
    outs = [refs.pop(0) for _ in range(2 if pair else 1)]
    stay_ref = refs.pop(0) if first else None
    next_ref = None if last else refs.pop(0)
    weights, partial, sems, next_sems = refs[:4]
    hidden_sems = refs[4] if first else None

    local, sources, capacity, depth = hidden_ref.shape
    blocks = len(BLOCKS)
    width = partial.shape[2] // blocks
    mine, rank = ids_ref[0], ids_ref[1]
    ahead = 0 if first else held_ref.shape[0]

    def strip(which, expert, q, target, sem):
        dest = lax.bitwise_xor(rank, BLOCKS[q])
        start = pl.multiple_of((dest * chunks + which) * width, LANES)
        return pltpu.make_async_copy(
            weight_ref.at[expert, :, pl.ds(start, width)], target.at[:, pl.ds(q * width, width)], sem
        )

    def bring(expert):
        at = expert - ahead
        return [strip(chunk, expert, q, weights.at[at], sems.at[at, q]) for q in range(blocks)]

    def bring_next(expert):
        return [strip(chunk + 1, expert, q, next_ref.at[expert], next_sems.at[expert, q]) for q in range(blocks)]

    def bring_hidden(expert):
        return pltpu.make_async_copy(hidden_ref.at[expert], stay_ref.at[expert], hidden_sems.at[expert])

    for expert in range(local):
        if first:
            bring_hidden(expert).start()
        if expert >= ahead:
            for copy in bring(expert):
                copy.start()
    if not last:
        for expert in range(next_ref.shape[0]):
            for copy in bring_next(expert):
                copy.start()

    for expert in range(local):
        if first:
            bring_hidden(expert).wait()
        if expert >= ahead:
            for copy in bring(expert):
                copy.wait()
            weight = weights[expert - ahead]
        else:
            weight = held_ref[expert]
        rows = (stay_ref if first else hidden_ref)[expert].reshape(sources * capacity, depth)
        product = jnp.dot(rows, weight, preferred_element_type=jnp.float32).astype(partial.dtype)
        for source in range(sources):
            partial[source, expert * capacity : (expert + 1) * capacity, :] = product[
                source * capacity : (source + 1) * capacity
            ]

    def combine(source):
        total = jnp.dot(table_ref[source], partial[source], preferred_element_type=jnp.float32)
        return total.astype(outs[0].dtype)

    if pair:
        for out_ref, source in zip(outs, (1 - mine, mine)):
            total = combine(source)
            for q in range(blocks):
                out_ref[q] = total[:, q * width : (q + 1) * width]
    else:
        for source in range(sources):
            total = combine(source)
            for q in range(blocks):
                outs[0][source, q] = total[:, q * width : (q + 1) * width]
    if not last:
        for expert in range(next_ref.shape[0]):
            for copy in bring_next(expert):
                copy.wait()


def chunk_sums(chunk, chunks, pair, ids, hidden, weight, table, held):
    first, last = chunk == 0, chunk == chunks - 1
    local, sources, capacity, depth = hidden.shape
    tokens = table.shape[1]
    blocks = len(BLOCKS)
    width = weight.shape[2] // (blocks * chunks)
    ahead = min(AHEAD, local)
    brought = local if first else local - ahead
    bf16 = jnp.bfloat16
    group = jax.ShapeDtypeStruct((blocks, tokens, width), bf16)
    if pair:
        out_shape = [group, group]
    else:
        out_shape = [jax.ShapeDtypeStruct((sources, blocks, tokens, width), bf16)]
    if first:
        out_shape.append(jax.ShapeDtypeStruct(hidden.shape, bf16))
    if not last:
        out_shape.append(jax.ShapeDtypeStruct((ahead, depth, blocks * width), bf16))
    scratch = [
        pltpu.VMEM((max(brought, 1), depth, blocks * width), bf16),
        pltpu.VMEM((sources, local * capacity, blocks * width), bf16),
        pltpu.SemaphoreType.DMA((max(brought, 1), blocks)),
        pltpu.SemaphoreType.DMA((ahead, blocks)),
    ]
    if first:
        scratch.append(pltpu.SemaphoreType.DMA((local,)))
    operands = [ids, hidden, weight, table] + ([] if first else [held])
    flops = 2 * sources * local * capacity * blocks * width * (depth + tokens)
    results = pl.pallas_call(
        functools.partial(chunk_kernel, chunk, chunks, pair),
        in_specs=[SMEM, ANY if first else VMEM, ANY, VMEM] + ([] if first else [VMEM]),
        out_specs=[VMEM] * len(out_shape),
        out_shape=out_shape,
        scratch_shapes=scratch,
        cost_estimate=pl.CostEstimate(
            flops=flops, bytes_accessed=2 * local * depth * blocks * width, transcendentals=0
        ),
        compiler_params=pltpu.CompilerParams(vmem_limit_bytes=32 << 20),
        name=f"chunk{chunk}",
    )(*operands)
    results = list(results)
    sums = [results.pop(0) for _ in range(2 if pair else 1)]
    hidden = results.pop(0) if first else hidden
    held = None if last else results.pop(0)
    return sums, hidden, held


def on_device(experts, ranks, hidden, down_weight, routes, route_weight, residual):
    f32, bf16 = jnp.float32, jnp.bfloat16
    local, sources, capacity, _ = hidden.shape
    tokens = routes.shape[0]
    pair = experts == 2
    me, rank = lax.axis_index("expert"), lax.axis_index("tp")
    ids = jnp.stack([me, rank]).astype(jnp.int32)
    if pair:
        swap = [(0, 1), (1, 0)]
        other_routes = lax.ppermute(routes, "expert", swap)
        other_weight = lax.ppermute(route_weight, "expert", swap)

        def by_source(own, other):
            return jnp.where(me == 0, jnp.stack([own, other]), jnp.stack([other, own]))

        all_routes, all_weight = by_source(routes, other_routes), by_source(route_weight, other_weight)
    else:
        all_routes = lax.all_gather(routes, "expert").reshape(sources, -1, routes.shape[1])
        all_weight = lax.all_gather(route_weight, "expert").reshape(sources, -1, routes.shape[1])
    table = share_tables(ids, all_routes, all_weight, local, capacity)

    features = residual.shape[1]
    chunks = features // LANES
    near = [(i, i ^ 1) for i in range(ranks)]
    far = [(i, i ^ 2) for i in range(ranks)]
    held, pieces = None, []
    for chunk in range(chunks):
        sums, hidden, held = chunk_sums(chunk, chunks, pair, ids, hidden, down_weight, table, held)
        if pair:
            other, own = sums
            got = lax.ppermute(other, "expert", swap)
            send = (own[:2].astype(f32) + got[:2].astype(f32)).astype(bf16)
            base = own[2:].astype(f32) + got[2:].astype(f32)
        else:
            whole = lax.psum_scatter(sums[0], "expert", scatter_dimension=0, tiled=True)
            whole = jnp.moveaxis(whole, 0, 1).reshape(len(BLOCKS), tokens, LANES)
            send, base = whole[:2], whole[2:].astype(f32)
        near_got = lax.ppermute(send, "tp", near).astype(f32)
        far_got = lax.ppermute((base[0] + near_got[0]).astype(bf16), "tp", far).astype(f32)
        here = residual[:, chunk * LANES : (chunk + 1) * LANES].astype(f32)
        pieces.append((here + (base[1] + near_got[1] + far_got)).astype(bf16))
    return jnp.concatenate(pieces, axis=1)


def solution(mesh):
    return jax.shard_map(
        functools.partial(on_device, mesh.shape["expert"], mesh.shape["tp"]),
        mesh=mesh,
        in_specs=(
            P("expert", "dp", None, "tp"),
            P("expert", "tp", None),
            P(("dp", "expert"), None),
            P(("dp", "expert"), None),
            P(("dp", "expert"), "tp"),
        ),
        out_specs=P(("dp", "expert"), "tp"),
        check_vma=False,
    )
```

```python
import functools

import jax
import jax.numpy as jnp
from jax import lax
from jax.experimental import pallas as pl
from jax.experimental.pallas import tpu as pltpu
from jax.sharding import PartitionSpec as P

LANES = 128
AHEAD = 2
BLOCKS = (3, 1, 2, 0)
WIDTHS = (1, 2, 2, 1)

VMEM = pl.BlockSpec(memory_space=pltpu.VMEM)
SMEM = pl.BlockSpec(memory_space=pltpu.SMEM)
ANY = pl.BlockSpec(memory_space=pl.ANY)
HBM = pl.BlockSpec(memory_space=pltpu.HBM)
BF16 = jnp.bfloat16


def strips(ids_ref, weight_ref, chunk, expert, target, sems):
    start, width, features = chunk
    rank = ids_ref[1]
    copies = []
    for q, flip in enumerate(BLOCKS):
        at = pl.multiple_of(lax.bitwise_xor(rank, flip) * features + start, LANES)
        source = weight_ref.at[expert, :, pl.ds(at, width)]
        copies.append(pltpu.make_async_copy(source, target.at[:, pl.ds(q * width, width)], sems.at[q]))
    return copies


def product(rows_ref, weight, partial, expert):
    sources, capacity, depth = rows_ref.shape
    rows = rows_ref[...].reshape(sources * capacity, depth)
    value = jnp.dot(rows, weight, preferred_element_type=jnp.float32).astype(partial.dtype)
    for source in range(sources):
        partial[source, expert * capacity : (expert + 1) * capacity, :] = value[
            source * capacity : (source + 1) * capacity
        ]


def combine(ids_ref, table_ref, partial, outs):
    sources = table_ref.shape[0]
    width = partial.shape[2] // len(BLOCKS)
    mine = ids_ref[0]
    pair = len(outs) == 2
    order = [(outs[0], 1 - mine), (outs[1], mine)] if pair else [(outs[0].at[s], s) for s in range(sources)]
    for out_ref, source in order:
        total = jnp.dot(table_ref[source], partial[source], preferred_element_type=jnp.float32)
        total = total.astype(out_ref.dtype)
        for q in range(len(BLOCKS)):
            out_ref[q] = total[:, q * width : (q + 1) * width]


def first_kernel(chunk, ids_ref, hidden_ref, weight_ref, partial, stay_ref, weights, sems, hidden_sems):
    local = hidden_ref.shape[0]

    def bring(expert):
        copy = pltpu.make_async_copy(hidden_ref.at[expert], stay_ref.at[expert], hidden_sems.at[expert])
        return [copy] + strips(ids_ref, weight_ref, chunk, expert, weights.at[expert], sems.at[expert])

    for expert in range(local):
        for copy in bring(expert):
            copy.start()
    for expert in range(local):
        for copy in bring(expert):
            copy.wait()
        product(stay_ref.at[expert], weights[expert], partial, expert)


def table_kernel(chunk, capacity, groups, *refs):
    refs = list(refs)
    ids_ref, partial, weight_ref = refs[:3]
    routes_refs, score_refs = refs[3 : 3 + groups], refs[3 + groups : 3 + 2 * groups]
    table_ref, *outs, next_ref, next_sems = refs[3 + 2 * groups :]
    sources, tokens, width = table_ref.shape
    local = width // capacity
    f32 = jnp.float32
    mine = ids_ref[0]
    first = mine * local
    copies = [
        strips(ids_ref, weight_ref, chunk, expert, next_ref.at[expert], next_sems.at[expert])
        for expert in range(next_ref.shape[0])
    ]
    for copy in sum(copies, []):
        copy.start()

    rows = lax.broadcasted_iota(jnp.int32, (tokens, tokens), 0)
    cols = lax.broadcasted_iota(jnp.int32, (tokens, tokens), 1)
    earlier = (rows < cols).astype(f32).astype(BF16)
    if groups == 2:
        parts = [(routes_refs[1][...], score_refs[1][...], 1 - mine), (routes_refs[0][...], score_refs[0][...], mine)]
    else:
        parts = [(routes_refs[0][s], score_refs[0][s], s) for s in range(sources)]
    for routes, score, source in parts:
        top = routes.shape[0]
        share = score / jnp.sum(score, axis=0, keepdims=True)
        experts = lax.broadcasted_iota(jnp.int32, (LANES // 8, tokens), 0)
        matches = [(experts == routes[k : k + 1]).astype(f32) for k in range(top)]
        onehot = functools.reduce(jnp.add, matches)
        before = jnp.dot(onehot.astype(BF16), earlier, preferred_element_type=f32)
        places = lax.broadcasted_iota(jnp.int32, (width, tokens), 0)
        entry = jnp.zeros((width, tokens), f32)
        for k in range(top):
            slot = jnp.sum(matches[k] * before, axis=0, keepdims=True).astype(jnp.int32)
            expert = routes[k : k + 1] - first
            at = jnp.where((expert >= 0) & (expert < local), expert * capacity + slot, -1)
            entry = jnp.where(places == at, share[k : k + 1], entry)
        table_ref[source] = entry.T.astype(table_ref.dtype)
    combine(ids_ref, table_ref, partial, outs)
    for copy in sum(copies, []):
        copy.wait()


def chunk_kernel(chunk, following, pair, ids_ref, hidden_ref, weight_ref, table_ref, held_ref, *refs):
    refs = list(refs[1:])
    outs = [refs.pop(0) for _ in range(2 if pair else 1)]
    next_ref = refs.pop(0) if following else None
    weights, partial, sems, next_sems = refs
    local, ahead = hidden_ref.shape[0], held_ref.shape[0]

    def bring(expert):
        at = expert - ahead
        return strips(ids_ref, weight_ref, chunk, expert, weights.at[at], sems.at[at])

    def bring_next(expert):
        return strips(ids_ref, weight_ref, following, expert, next_ref.at[expert], next_sems.at[expert])

    for expert in range(ahead, local):
        for copy in bring(expert):
            copy.start()
    if following:
        for expert in range(ahead):
            for copy in bring_next(expert):
                copy.start()
    for expert in range(local):
        if expert >= ahead:
            for copy in bring(expert):
                copy.wait()
            product(hidden_ref.at[expert], weights[expert - ahead], partial, expert)
        else:
            product(hidden_ref.at[expert], held_ref[expert], partial, expert)
    combine(ids_ref, table_ref, partial, outs)
    if following:
        for expert in range(ahead):
            for copy in bring_next(expert):
                copy.wait()


def shape(*dims):
    return jax.ShapeDtypeStruct(dims, BF16)


def cost(flops, *arrays):
    return pl.CostEstimate(flops=flops, bytes_accessed=sum(2 * a for a in arrays), transcendentals=0)


def first_products(chunk, ids, hidden, weight):
    local, sources, capacity, depth = hidden.shape
    columns = len(BLOCKS) * chunk[1]
    rows = local * sources * capacity
    return pl.pallas_call(
        functools.partial(first_kernel, chunk),
        in_specs=[SMEM, HBM, HBM],
        out_specs=[VMEM] * 2,
        out_shape=[shape(sources, local * capacity, columns), shape(*hidden.shape)],
        scratch_shapes=[
            pltpu.VMEM((local, depth, columns), BF16),
            pltpu.SemaphoreType.DMA((local, len(BLOCKS))),
            pltpu.SemaphoreType.DMA((local,)),
        ],
        cost_estimate=cost(2 * rows * depth * columns, local * depth * columns, rows * depth),
        compiler_params=pltpu.CompilerParams(vmem_limit_bytes=48 << 20),
        name="first",
    )(ids, hidden, weight)


def group_shapes(pair, sources, tokens, width):
    group = (len(BLOCKS), tokens, width)
    return [shape(*group)] * 2 if pair else [shape(sources, *group)]


def tables(chunk, following, pair, ids, partial, weight, routes, scores, capacity):
    sources, width, columns = partial.shape
    tokens = routes[0].shape[-1]
    depth = weight.shape[1]
    ahead = min(AHEAD, width // capacity)
    outs = group_shapes(pair, sources, tokens, chunk[1])
    table, *sums, held = pl.pallas_call(
        functools.partial(table_kernel, following, capacity, len(routes)),
        in_specs=[SMEM, VMEM, HBM] + [VMEM] * (2 * len(routes)),
        out_specs=[VMEM] * (len(outs) + 2),
        out_shape=[shape(sources, tokens, width)] + outs + [shape(ahead, depth, len(BLOCKS) * following[1])],
        scratch_shapes=[pltpu.SemaphoreType.DMA((ahead, len(BLOCKS)))],
        cost_estimate=cost(2 * sources * tokens * width * columns, ahead * depth * columns),
        compiler_params=pltpu.CompilerParams(vmem_limit_bytes=24 << 20),
        name="tables",
    )(ids, partial, weight, *routes, *scores)
    return table, sums, held


def chunk_sums(chunk, following, pair, ids, hidden, weight, table, held, after):
    local, sources, capacity, depth = hidden.shape
    tokens = table.shape[1]
    columns = len(BLOCKS) * chunk[1]
    ahead = held.shape[0]
    brought = max(local - ahead, 1)
    outs = group_shapes(pair, sources, tokens, chunk[1])
    groups = len(outs)
    if following:
        outs.append(shape(ahead, depth, len(BLOCKS) * following[1]))
    rows = sources * local * capacity
    results = pl.pallas_call(
        functools.partial(chunk_kernel, chunk, following, pair),
        in_specs=[SMEM, VMEM, HBM, VMEM, VMEM, ANY],
        out_specs=[VMEM] * len(outs),
        out_shape=outs,
        scratch_shapes=[
            pltpu.VMEM((brought, depth, columns), BF16),
            pltpu.VMEM((sources, local * capacity, columns), BF16),
            pltpu.SemaphoreType.DMA((brought, len(BLOCKS))),
            pltpu.SemaphoreType.DMA((ahead, len(BLOCKS))),
        ],
        cost_estimate=cost(2 * rows * columns * (depth + tokens), local * depth * columns),
        compiler_params=pltpu.CompilerParams(vmem_limit_bytes=28 << 20),
        name="chunk",
    )(ids, hidden, weight, table, held, after)
    return results[:groups], results[groups] if following else None


def on_device(experts, ranks, hidden, down_weight, routes, route_weight, residual):
    f32 = jnp.float32
    capacity = hidden.shape[2]
    tokens, features = residual.shape
    pair = experts == 2
    ids = jnp.stack([lax.axis_index("expert"), lax.axis_index("tp")]).astype(jnp.int32)
    routes, scores = routes.T, route_weight.T
    swap = [(0, 1), (1, 0)]
    if pair:
        all_routes = [routes, lax.ppermute(routes, "expert", swap)]
        all_scores = [scores, lax.ppermute(scores, "expert", swap)]
    else:
        all_routes = [lax.all_gather(routes, "expert")]
        all_scores = [lax.all_gather(scores, "expert")]

    near = [(i, i ^ 1) for i in range(ranks)]
    far = [(i, i ^ 2) for i in range(ranks)]
    chunks, start = [], 0
    for width in WIDTHS:
        chunks.append((start, width * LANES, features))
        start += width * LANES
    partial, hidden = first_products(chunks[0], ids, hidden, down_weight)
    table, sums, held = tables(
        chunks[0], chunks[1], pair, ids, partial, down_weight, all_routes, all_scores, capacity
    )
    pieces, sent = [], []
    for i, (start, width, _) in enumerate(chunks):
        if i:
            following = chunks[i + 1] if i + 1 < len(chunks) else None
            after = sent[i - 2] if i > 1 else ids
            sums, held = chunk_sums(chunks[i], following, pair, ids, hidden, down_weight, table, held, after)
        if pair:
            other, own = sums
            got = lax.ppermute(other, "expert", swap)
            send = (own[:2].astype(f32) + got[:2].astype(f32)).astype(BF16)
            base = own[2:].astype(f32) + got[2:].astype(f32)
        else:
            whole = lax.psum_scatter(sums[0], "expert", scatter_dimension=0, tiled=True)
            whole = jnp.moveaxis(whole, 0, 1).reshape(len(BLOCKS), tokens, width)
            send, base = whole[:2], whole[2:].astype(f32)
        sent.append(send)
        near_got = lax.ppermute(send, "tp", near).astype(f32)
        far_got = lax.ppermute((base[0] + near_got[0]).astype(BF16), "tp", far).astype(f32)
        here = residual[:, start : start + width].astype(f32)
        pieces.append((here + (base[1] + near_got[1] + far_got)).astype(BF16))
    return jnp.concatenate(pieces, axis=1)


def solution(mesh):
    return jax.shard_map(
        functools.partial(on_device, mesh.shape["expert"], mesh.shape["tp"]),
        mesh=mesh,
        in_specs=(
            P("expert", "dp", None, "tp"),
            P("expert", "tp", None),
            P(("dp", "expert"), None),
            P(("dp", "expert"), None),
            P(("dp", "expert"), "tp"),
        ),
        out_specs=P(("dp", "expert"), "tp"),
        check_vma=False,
    )
```

```python
import functools

import jax
import jax.numpy as jnp
from jax import lax
from jax.experimental import pallas as pl
from jax.experimental.pallas import tpu as pltpu
from jax.sharding import PartitionSpec as P

LANES = 128
TILE = 256
AHEAD = 2
WINDOW = 4
CHUNKS = (((3, 0, 3),), ((2, 0, 3), (1, 0, 1)), ((1, 1, 3), (0, 0, 1)), ((0, 1, 3),))

LATE = 10**10

VMEM = pl.BlockSpec(memory_space=pltpu.VMEM)
SMEM = pl.BlockSpec(memory_space=pltpu.SMEM)
ANY = pl.BlockSpec(memory_space=pl.ANY)
HBM = pl.BlockSpec(memory_space=pltpu.HBM)
BF16 = jnp.bfloat16


class Strips:
    def __init__(self, ids_ref, weight_ref, chunk, expert, target, sem):
        self.rank, self.weight_ref, self.chunk = ids_ref[1], weight_ref.at[expert], chunk
        self.target, self.sem = target, sem

    def start(self):
        column = 0
        for block, start, stop, features in self.chunk:
            at = pl.multiple_of(lax.bitwise_xor(self.rank, block) * features + start, LANES)
            target = self.target.at[:, pl.ds(column, stop - start)]
            pltpu.make_async_copy(self.weight_ref.at[:, pl.ds(at, stop - start)], target, self.sem).start()
            column += stop - start

    def wait(self):
        pltpu.make_async_copy(self.weight_ref.at[:, pl.ds(0, self.target.shape[1])], self.target, self.sem).wait()


def columns_of(chunk):
    return sum(stop - start for _, start, stop, _ in chunk)


def balanced_dot(rows, weight_ref, finish):
    depth, width = weight_ref.shape
    even = width // TILE // 2 * 2 * TILE
    half = -(-depth // 2 // TILE) * TILE
    if width - even != TILE or half >= depth:
        even = width
    f32 = jnp.float32
    finish(0, even, jnp.dot(rows, weight_ref[:, :even], preferred_element_type=f32))
    if even < width:
        low = jnp.dot(rows[:, :half], weight_ref[:half, even:], preferred_element_type=f32)
        high = jnp.dot(rows[:, half:], weight_ref[half:, even:], preferred_element_type=f32)
        finish(even, width, low + high)


def product(rows_ref, weight_ref, partial, expert):
    sources, capacity, depth = rows_ref.shape

    def finish(start, stop, value):
        value = value.astype(partial.dtype)
        for source in range(sources):
            partial[source, expert * capacity : (expert + 1) * capacity, start:stop] = value[
                source * capacity : (source + 1) * capacity
            ]

    balanced_dot(rows_ref[...].reshape(sources * capacity, depth), weight_ref, finish)


def combine(ids_ref, table_refs, partial, outs):
    mine = ids_ref[0]
    if len(outs) == 2:
        order = [(outs[0], table_refs[0], 1 - mine), (outs[1], table_refs[1], mine)]
    else:
        order = [(outs[0].at[s], table_refs[0].at[s], s) for s in range(partial.shape[0])]
    for out_ref, table_ref, source in order:

        def finish(start, stop, value, out_ref=out_ref):
            out_ref[:, start:stop] = value.astype(out_ref.dtype)

        balanced_dot(table_ref[...], partial.at[source], finish)


def share_table(ids_ref, routes, score, local, capacity):
    f32 = jnp.float32
    top, tokens = routes.shape
    width = local * capacity
    first = ids_ref[0] * local
    rows = lax.broadcasted_iota(jnp.int32, (tokens, tokens), 0)
    cols = lax.broadcasted_iota(jnp.int32, (tokens, tokens), 1)
    earlier = (rows < cols).astype(f32).astype(BF16)
    share = score / jnp.sum(score, axis=0, keepdims=True)
    experts = lax.broadcasted_iota(jnp.int32, (LANES // 8, tokens), 0)
    matches = [(experts == routes[k : k + 1]).astype(f32) for k in range(top)]
    onehot = functools.reduce(jnp.add, matches)
    before = jnp.dot(onehot.astype(BF16), earlier, preferred_element_type=f32)
    places = lax.broadcasted_iota(jnp.int32, (width, tokens), 0)
    entry = jnp.zeros((width, tokens), f32)
    for k in range(top):
        slot = jnp.sum(matches[k] * before, axis=0, keepdims=True).astype(jnp.int32)
        expert = routes[k : k + 1] - first
        at = jnp.where((expert >= 0) & (expert < local), expert * capacity + slot, -1)
        entry = jnp.where(places == at, share[k : k + 1], entry)
    return entry.T.astype(BF16)


class Stream:
    def __init__(self, groups):
        self.groups, self.begun, self.ended = groups, 0, 0
        for _ in range(WINDOW):
            self.begin()

    def begin(self):
        if self.begun < len(self.groups):
            for copy in self.groups[self.begun]:
                copy.start()
            self.begun += 1

    def end(self):
        for copy in self.groups[self.ended]:
            copy.wait()
        self.ended += 1
        self.begin()

    def finish(self):
        while self.ended < len(self.groups):
            self.end()


def first_kernel(chunk, ids_ref, hidden_ref, weight_ref, partial, stay_ref, weights, sems, hidden_sems):
    def bring(expert):
        copy = pltpu.make_async_copy(hidden_ref.at[expert], stay_ref.at[expert], hidden_sems.at[expert])
        return [copy, Strips(ids_ref, weight_ref, chunk, expert, weights.at[expert], sems.at[expert])]

    local = hidden_ref.shape[0]
    stream = Stream([bring(expert) for expert in range(local)])
    for expert in range(local):
        stream.end()
        product(stay_ref.at[expert], weights.at[expert], partial, expert)


def table_kernel(chunk, pair, capacity, *refs):
    refs = list(refs)
    ids_ref, partial, weight_ref = refs[:3]
    count = 2 if pair else 1
    routes_refs, score_refs, table_refs = refs[3 : 3 + count], refs[3 + count : 3 + 2 * count], refs[3 + 2 * count :]
    outs, (next_ref, next_sems) = table_refs[count:-2], table_refs[-2:]
    table_refs = table_refs[:count]
    local = table_refs[0].shape[-1] // capacity
    stream = Stream(
        [
            [Strips(ids_ref, weight_ref, chunk, expert, next_ref.at[expert], next_sems.at[expert])]
            for expert in range(next_ref.shape[0])
        ]
    )
    for routes_ref, score_ref, table_ref in zip(routes_refs, score_refs, table_refs):
        if pair:
            table_ref[...] = share_table(ids_ref, routes_ref[...], score_ref[...], local, capacity)
        else:
            for s in range(table_ref.shape[0]):
                table_ref[s] = share_table(ids_ref, routes_ref[s], score_ref[s], local, capacity)
    combine(ids_ref, table_refs, partial, outs)
    stream.finish()


def chunk_kernel(chunk, following, groups, ids_ref, hidden_ref, weight_ref, held_ref, *refs):
    refs = list(refs)
    table_refs = [refs.pop(0) for _ in range(groups)]
    del refs[0]
    outs = [refs.pop(0) for _ in range(groups)]
    next_ref = refs.pop(0) if following else None
    weights, partial, sems, next_sems = refs
    local, ahead = hidden_ref.shape[0], held_ref.shape[0]

    own = [
        [Strips(ids_ref, weight_ref, chunk, e, weights.at[e - ahead], sems.at[e - ahead])]
        for e in range(ahead, local)
    ]
    later = [
        [Strips(ids_ref, weight_ref, following, e, next_ref.at[e], next_sems.at[e])]
        for e in range(ahead if following else 0)
    ]
    stream = Stream(own + later)
    for expert in range(local):
        if expert >= ahead:
            stream.end()
            product(hidden_ref.at[expert], weights.at[expert - ahead], partial, expert)
        else:
            product(hidden_ref.at[expert], held_ref.at[expert], partial, expert)
    combine(ids_ref, table_refs, partial, outs)
    stream.finish()


def fold_kernel(spans, *refs):
    *terms, _, sum_ref = refs
    edges = sorted({edge for _, at, width in spans for edge in (at, at + width)})
    for low, high in zip(edges[:-1], edges[1:]):
        parts = [
            term[:, source + low - at : source + high - at].astype(jnp.float32)
            for term, (source, at, width) in zip(terms, spans)
            if at <= low < at + width
        ]
        sum_ref[:, low:high] = functools.reduce(jnp.add, parts).astype(sum_ref.dtype)


def shape(*dims):
    return jax.ShapeDtypeStruct(dims, BF16)


def cost(flops, count):
    return pl.CostEstimate(flops=flops, bytes_accessed=2 * count, transcendentals=0)


COST = cost(1000, 1000)


def first_products(chunk, ids, hidden, weight):
    local, sources, capacity, depth = hidden.shape
    columns = columns_of(chunk)
    return pl.pallas_call(
        functools.partial(first_kernel, chunk),
        in_specs=[SMEM, HBM, HBM],
        out_specs=[VMEM] * 2,
        out_shape=[shape(sources, local * capacity, columns), shape(*hidden.shape)],
        scratch_shapes=[
            pltpu.VMEM((local, depth, columns), BF16),
            pltpu.SemaphoreType.DMA((local,)),
            pltpu.SemaphoreType.DMA((local,)),
        ],
        cost_estimate=cost(2 * sources * local * capacity * columns * depth, local * depth * columns),
        compiler_params=pltpu.CompilerParams(vmem_limit_bytes=46 << 20),
        name="first",
    )(ids, hidden, weight)


def group_shapes(pair, sources, tokens, width):
    return [shape(tokens, width)] * 2 if pair else [shape(sources, tokens, width)]


def tables(following, ids, partial, weight, routes, scores, capacity):
    sources, width, columns = partial.shape
    pair = len(routes) == 2
    tokens = routes[0].shape[-1]
    depth = weight.shape[1]
    ahead = min(AHEAD, width // capacity)
    table = [shape(tokens, width)] * 2 if pair else [shape(sources, tokens, width)]
    outs = group_shapes(pair, sources, tokens, columns)
    results = pl.pallas_call(
        functools.partial(table_kernel, following, pair, capacity),
        in_specs=[SMEM, VMEM, HBM] + [VMEM] * (2 * len(routes)),
        out_specs=[VMEM] * (len(table) + len(outs) + 1),
        out_shape=table + outs + [shape(ahead, depth, columns_of(following))],
        scratch_shapes=[pltpu.SemaphoreType.DMA((ahead,))],
        cost_estimate=COST,
        compiler_params=pltpu.CompilerParams(vmem_limit_bytes=12 << 20),
        name="tables",
    )(ids, partial, weight, *routes, *scores)
    return results[: len(table)], results[len(table) : -1], results[-1]


def chunk_sums(chunk, following, ids, hidden, weight, table, held, after):
    local, sources, capacity, depth = hidden.shape
    tokens = table[0].shape[-2]
    ahead, _, columns = held.shape
    brought = max(local - ahead, 1)
    groups = len(table)
    outs = group_shapes(groups == 2, sources, tokens, columns)
    if following:
        outs.append(shape(ahead, depth, columns_of(following)))
    flops = 2 * sources * local * capacity * columns * (depth + tokens)
    results = pl.pallas_call(
        functools.partial(chunk_kernel, chunk, following, groups),
        in_specs=[SMEM, VMEM, HBM, VMEM] + [VMEM] * groups + [ANY],
        out_specs=[VMEM] * len(outs),
        out_shape=outs,
        scratch_shapes=[
            pltpu.VMEM((brought, depth, columns), BF16),
            pltpu.VMEM((sources, local * capacity, columns), BF16),
            pltpu.SemaphoreType.DMA((brought,)),
            pltpu.SemaphoreType.DMA((ahead,)),
        ],
        cost_estimate=cost(flops, local * depth * columns) if following else COST,
        compiler_params=pltpu.CompilerParams(vmem_limit_bytes=28 << 20),
        name="chunk",
    )(ids, hidden, weight, held, *table, after)
    return results[:groups], results[groups] if following else None


def fold(width, terms, after, dtype=BF16, flops=1000):
    arrays, spans = [term[0] for term in terms], [term[1:] for term in terms]
    return pl.pallas_call(
        functools.partial(fold_kernel, spans),
        in_specs=[VMEM] * len(terms) + [ANY],
        out_specs=VMEM,
        out_shape=jax.ShapeDtypeStruct((arrays[0].shape[0], width), dtype),
        cost_estimate=cost(flops, 1000),
        compiler_params=pltpu.CompilerParams(vmem_limit_bytes=6 << 20),
        name="fold",
    )(*arrays, after)


def on_device(experts, ranks, hidden, down_weight, routes, route_weight, residual):
    f32 = jnp.float32
    capacity = hidden.shape[2]
    tokens, features = residual.shape
    pair = experts == 2
    ids = jnp.stack([lax.axis_index("expert"), lax.axis_index("tp")]).astype(jnp.int32)
    routes, scores = routes.T, route_weight.T
    swap = [(0, 1), (1, 0)]
    if pair:
        routes, scores = [lax.ppermute(routes, "expert", swap), routes], [lax.ppermute(scores, "expert", swap), scores]
    else:
        routes, scores = [lax.all_gather(routes, "expert")], [lax.all_gather(scores, "expert")]

    chunks = [
        tuple((block, start * features // 3, stop * features // 3, features) for block, start, stop in chunk)
        for chunk in CHUNKS
    ]
    over, along = [], {}

    def send_over(sums):
        if pair:
            over.append([sums[1], lax.ppermute(sums[0], "expert", swap)])
        else:
            whole = lax.psum_scatter(sums[0], "expert", scatter_dimension=0, tiled=True)
            over.append([whole.reshape(tokens, -1)])

    def terms(i, block, base):
        column = 0
        for which, start, stop, _ in chunks[i]:
            if which == block:
                found = [(array, column, start - base, stop - start) for array in over[i]]
                for array, first, width in along.get(block, []):
                    low, high = max(start, first), min(stop, first + width)
                    if low < high:
                        found.append((array, low - first, low - base, high - low))
                return found
            column += stop - start

    def send_along(i, block, flip, after):
        start, stop = next((start, stop) for which, start, stop, _ in chunks[i] if which == block)
        total = fold(stop - start, terms(i, block, start), after)
        got = lax.ppermute(total, "tp", [(r, r ^ flip) for r in range(ranks)])
        along.setdefault(block ^ flip, []).append((got, start, stop - start))
        return total

    partial, hidden = first_products(chunks[0], ids, hidden, down_weight)
    table, sums, held = tables(chunks[1], ids, partial, down_weight, routes, scores, capacity)
    send_over(sums)
    sums, held = chunk_sums(chunks[1], chunks[2], ids, hidden, down_weight, table, held, ids)
    send_over(sums)
    total = send_along(0, 3, 1, sums[0])
    sums, held = chunk_sums(chunks[2], chunks[3], ids, hidden, down_weight, table, held, total)
    send_over(sums)
    total = send_along(1, 2, 2, sums[0])
    total = send_along(1, 1, 1, total)
    sums, _ = chunk_sums(chunks[3], None, ids, hidden, down_weight, table, held, total)
    send_over(sums)
    send_along(2, 1, 1, sums[0])
    far, near, last = [(array, 0, first, width) for array, first, width in along[0]]
    here = [(residual, 0, 0, features)]
    rest = fold(features, here + [far, near] + [(a, c, at, w) for a, c, at, w in terms(2, 0, 0)[: len(over[2])]], ids, f32, LATE)
    rest = fold(features, [(rest, 0, 0, features)] + terms(3, 0, 0)[: len(over[3])], ids, f32, LATE)
    return fold(features, [(rest, 0, 0, features), last], ids)


def solution(mesh):
    return jax.shard_map(
        functools.partial(on_device, mesh.shape["expert"], mesh.shape["tp"]),
        mesh=mesh,
        in_specs=(
            P("expert", "dp", None, "tp"),
            P("expert", "tp", None),
            P(("dp", "expert"), None),
            P(("dp", "expert"), None),
            P(("dp", "expert"), "tp"),
        ),
        out_specs=P(("dp", "expert"), "tp"),
        check_vma=False,
    )
```

```python
import functools

import jax
import jax.numpy as jnp
from jax import lax
from jax.experimental import pallas as pl
from jax.experimental.pallas import tpu as pltpu
from jax.sharding import PartitionSpec as P

LANES = 128
TILE = 256
AHEAD = (2, 4, 4)
WINDOW = 6
BLOCKS = (3, 2, 1, 0)

LATE = 10**10

VMEM = pl.BlockSpec(memory_space=pltpu.VMEM)
SMEM = pl.BlockSpec(memory_space=pltpu.SMEM)
ANY = pl.BlockSpec(memory_space=pl.ANY)
HBM = pl.BlockSpec(memory_space=pltpu.HBM)
BF16 = jnp.bfloat16


def strip(ids_ref, weight_ref, block, expert, target, sem):
    width = target.shape[1]
    at = pl.multiple_of(lax.bitwise_xor(ids_ref[1], block) * width, LANES)
    return pltpu.make_async_copy(weight_ref.at[expert, :, pl.ds(at, width)], target, sem)


def balanced_dot(rows, weight_ref, finish):
    depth, width = weight_ref.shape
    even = width // TILE // 2 * 2 * TILE
    half = -(-depth // 2 // TILE) * TILE
    if width - even != TILE or half >= depth:
        even = width
    f32 = jnp.float32
    finish(0, even, jnp.dot(rows, weight_ref[:, :even], preferred_element_type=f32))
    if even < width:
        low = jnp.dot(rows[:, :half], weight_ref[:half, even:], preferred_element_type=f32)
        high = jnp.dot(rows[:, half:], weight_ref[half:, even:], preferred_element_type=f32)
        finish(even, width, low + high)


def product(rows_ref, weight_ref, partial, expert):
    sources, capacity, depth = rows_ref.shape

    def finish(start, stop, value):
        value = value.astype(partial.dtype)
        for source in range(sources):
            partial[source, expert * capacity : (expert + 1) * capacity, start:stop] = value[
                source * capacity : (source + 1) * capacity
            ]

    balanced_dot(rows_ref[...].reshape(sources * capacity, depth), weight_ref, finish)


def combine(ids_ref, table_refs, partial, outs):
    mine = ids_ref[0]
    if len(outs) == 2:
        order = [(outs[0], table_refs[0], 1 - mine), (outs[1], table_refs[1], mine)]
    else:
        order = [(outs[0].at[s], table_refs[0].at[s], s) for s in range(partial.shape[0])]
    for out_ref, table_ref, source in order:

        def finish(start, stop, value, out_ref=out_ref):
            out_ref[:, start:stop] = value.astype(out_ref.dtype)

        balanced_dot(table_ref[...], partial.at[source], finish)


def share_table(ids_ref, routes, score, local, capacity):
    f32 = jnp.float32
    top, tokens = routes.shape
    width = local * capacity
    first = ids_ref[0] * local
    rows = lax.broadcasted_iota(jnp.int32, (tokens, tokens), 0)
    cols = lax.broadcasted_iota(jnp.int32, (tokens, tokens), 1)
    earlier = (rows < cols).astype(f32).astype(BF16)
    share = score / jnp.sum(score, axis=0, keepdims=True)
    experts = lax.broadcasted_iota(jnp.int32, (LANES // 8, tokens), 0)
    matches = [(experts == routes[k : k + 1]).astype(f32) for k in range(top)]
    onehot = functools.reduce(jnp.add, matches)
    before = jnp.dot(onehot.astype(BF16), earlier, preferred_element_type=f32)
    places = lax.broadcasted_iota(jnp.int32, (width, tokens), 0)
    entry = jnp.zeros((width, tokens), f32)
    for k in range(top):
        slot = jnp.sum(matches[k] * before, axis=0, keepdims=True).astype(jnp.int32)
        expert = routes[k : k + 1] - first
        at = jnp.where((expert >= 0) & (expert < local), expert * capacity + slot, -1)
        entry = jnp.where(places == at, share[k : k + 1], entry)
    return entry.T.astype(BF16)


class Stream:
    def __init__(self, groups):
        self.groups, self.begun, self.ended = groups, 0, 0
        for _ in range(WINDOW):
            self.begin()

    def begin(self):
        if self.begun < len(self.groups):
            for copy in self.groups[self.begun]:
                copy.start()
            self.begun += 1

    def end(self):
        for copy in self.groups[self.ended]:
            copy.wait()
        self.ended += 1
        self.begin()

    def finish(self):
        while self.ended < len(self.groups):
            self.end()


def first_kernel(block, ids_ref, hidden_ref, weight_ref, partial, stay_ref, weights, sems, hidden_sems):
    def bring(expert):
        copy = pltpu.make_async_copy(hidden_ref.at[expert], stay_ref.at[expert], hidden_sems.at[expert])
        return [copy, strip(ids_ref, weight_ref, block, expert, weights.at[expert], sems.at[expert])]

    local = hidden_ref.shape[0]
    stream = Stream([bring(expert) for expert in range(local)])
    for expert in range(local):
        stream.end()
        product(stay_ref.at[expert], weights.at[expert], partial, expert)


def table_kernel(block, pair, capacity, *refs):
    refs = list(refs)
    ids_ref, partial, weight_ref = refs[:3]
    count = 2 if pair else 1
    routes_refs, score_refs, table_refs = refs[3 : 3 + count], refs[3 + count : 3 + 2 * count], refs[3 + 2 * count :]
    outs, (next_ref, next_sems) = table_refs[count:-2], table_refs[-2:]
    table_refs = table_refs[:count]
    local = table_refs[0].shape[-1] // capacity
    stream = Stream(
        [
            [strip(ids_ref, weight_ref, block, expert, next_ref.at[expert], next_sems.at[expert])]
            for expert in range(next_ref.shape[0])
        ]
    )
    for routes_ref, score_ref, table_ref in zip(routes_refs, score_refs, table_refs):
        if pair:
            table_ref[...] = share_table(ids_ref, routes_ref[...], score_ref[...], local, capacity)
        else:
            for s in range(table_ref.shape[0]):
                table_ref[s] = share_table(ids_ref, routes_ref[s], score_ref[s], local, capacity)
    combine(ids_ref, table_refs, partial, outs)
    stream.finish()


def chunk_kernel(block, following, groups, ids_ref, hidden_ref, weight_ref, held_ref, *refs):
    refs = list(refs)
    table_refs = [refs.pop(0) for _ in range(groups)]
    del refs[0]
    outs = [refs.pop(0) for _ in range(groups)]
    next_ref = refs.pop(0) if following is not None else None
    weights, partial, sems, next_sems = refs
    local, ahead = hidden_ref.shape[0], held_ref.shape[0]

    own = [
        [strip(ids_ref, weight_ref, block, e, weights.at[e - ahead], sems.at[e - ahead])]
        for e in range(ahead, local)
    ]
    later = [
        [strip(ids_ref, weight_ref, following, e, next_ref.at[e], next_sems.at[e])]
        for e in range(next_ref.shape[0] if following is not None else 0)
    ]
    stream = Stream(own + later)
    for expert in range(local):
        if expert >= ahead:
            stream.end()
            product(hidden_ref.at[expert], weights.at[expert - ahead], partial, expert)
        else:
            product(hidden_ref.at[expert], held_ref.at[expert], partial, expert)
    combine(ids_ref, table_refs, partial, outs)
    stream.finish()


def fold_kernel(spans, *refs):
    *terms, _, sum_ref = refs
    edges = sorted({edge for _, at, width in spans for edge in (at, at + width)})
    for low, high in zip(edges[:-1], edges[1:]):
        parts = [
            term[:, source + low - at : source + high - at].astype(jnp.float32)
            for term, (source, at, width) in zip(terms, spans)
            if at <= low < at + width
        ]
        sum_ref[:, low:high] = functools.reduce(jnp.add, parts).astype(sum_ref.dtype)


def shape(*dims):
    return jax.ShapeDtypeStruct(dims, BF16)


def cost(flops, count):
    return pl.CostEstimate(flops=flops, bytes_accessed=2 * count, transcendentals=0)


COST = cost(1000, 1000)


def first_products(block, columns, ids, hidden, weight):
    local, sources, capacity, depth = hidden.shape
    return pl.pallas_call(
        functools.partial(first_kernel, block),
        in_specs=[SMEM, HBM, HBM],
        out_specs=[VMEM] * 2,
        out_shape=[shape(sources, local * capacity, columns), shape(*hidden.shape)],
        scratch_shapes=[
            pltpu.VMEM((local, depth, columns), BF16),
            pltpu.SemaphoreType.DMA((local,)),
            pltpu.SemaphoreType.DMA((local,)),
        ],
        cost_estimate=cost(2 * sources * local * capacity * columns * depth, local * depth * columns),
        compiler_params=pltpu.CompilerParams(vmem_limit_bytes=46 << 20),
        name="first",
    )(ids, hidden, weight)


def group_shapes(pair, sources, tokens, width):
    return [shape(tokens, width)] * 2 if pair else [shape(sources, tokens, width)]


def tables(following, ids, partial, weight, routes, scores, capacity):
    sources, width, columns = partial.shape
    pair = len(routes) == 2
    tokens = routes[0].shape[-1]
    depth = weight.shape[1]
    ahead = min(AHEAD[0], width // capacity)
    table = [shape(tokens, width)] * 2 if pair else [shape(sources, tokens, width)]
    outs = group_shapes(pair, sources, tokens, columns)
    results = pl.pallas_call(
        functools.partial(table_kernel, following, pair, capacity),
        in_specs=[SMEM, VMEM, HBM] + [VMEM] * (2 * len(routes)),
        out_specs=[VMEM] * (len(table) + len(outs) + 1),
        out_shape=table + outs + [shape(ahead, depth, columns)],
        scratch_shapes=[pltpu.SemaphoreType.DMA((ahead,))],
        cost_estimate=COST,
        compiler_params=pltpu.CompilerParams(vmem_limit_bytes=12 << 20),
        name="tables",
    )(ids, partial, weight, *routes, *scores)
    return results[: len(table)], results[len(table) : -1], results[-1]


def chunk_sums(block, following, ids, hidden, weight, table, held, after):
    local, sources, capacity, depth = hidden.shape
    tokens = table[0].shape[-2]
    ahead, _, columns = held.shape
    brought = max(local - ahead, 1)
    groups = len(table)
    outs = group_shapes(groups == 2, sources, tokens, columns)
    if following is not None:
        ahead_next = min(AHEAD[BLOCKS.index(block)], local)
        outs.append(shape(ahead_next, depth, columns))
    flops = 2 * sources * local * capacity * columns * (depth + tokens)
    results = pl.pallas_call(
        functools.partial(chunk_kernel, block, following, groups),
        in_specs=[SMEM, VMEM, HBM, VMEM] + [VMEM] * groups + [ANY],
        out_specs=[VMEM] * len(outs),
        out_shape=outs,
        scratch_shapes=[
            pltpu.VMEM((brought, depth, columns), BF16),
            pltpu.VMEM((sources, local * capacity, columns), BF16),
            pltpu.SemaphoreType.DMA((brought,)),
            pltpu.SemaphoreType.DMA((local,)),
        ],
        cost_estimate=cost(flops, local * depth * columns) if following is not None else COST,
        compiler_params=pltpu.CompilerParams(vmem_limit_bytes=20 << 20),
        name=f"chunk{block}",
    )(ids, hidden, weight, held, *table, after)
    return results[:groups], results[groups] if following is not None else None


def fold(width, terms, after, dtype=BF16, flops=1000):
    arrays, spans = [term[0] for term in terms], [term[1:] for term in terms]
    return pl.pallas_call(
        functools.partial(fold_kernel, spans),
        in_specs=[VMEM] * len(terms) + [ANY],
        out_specs=VMEM,
        out_shape=jax.ShapeDtypeStruct((arrays[0].shape[0], width), dtype),
        cost_estimate=cost(flops, 1000),
        compiler_params=pltpu.CompilerParams(vmem_limit_bytes=6 << 20),
        name="fold",
    )(*arrays, after)


def on_device(experts, ranks, hidden, down_weight, routes, route_weight, residual):
    f32 = jnp.float32
    capacity = hidden.shape[2]
    tokens, features = residual.shape
    pair = experts == 2
    ids = jnp.stack([lax.axis_index("expert"), lax.axis_index("tp")]).astype(jnp.int32)
    routes, scores = routes.T, route_weight.T
    swap = [(0, 1), (1, 0)]
    if pair:
        routes, scores = [lax.ppermute(routes, "expert", swap), routes], [lax.ppermute(scores, "expert", swap), scores]
    else:
        routes, scores = [lax.all_gather(routes, "expert")], [lax.all_gather(scores, "expert")]

    def send_over(sums, width=features):
        if pair:
            return [sums[1], lax.ppermute(sums[0][:, :width], "expert", swap)]
        return [lax.psum_scatter(sums[0], "expert", scatter_dimension=0, tiled=True).reshape(tokens, features)]

    def send_along(total, flip):
        return lax.ppermute(total, "tp", [(r, r ^ flip) for r in range(ranks)])

    def spans(arrays, width=features):
        return [(array, 0, 0, width) for array in arrays]

    partial, hidden = first_products(BLOCKS[0], features, ids, hidden, down_weight)
    table, sums, held = tables(BLOCKS[1], ids, partial, down_weight, routes, scores, capacity)
    over3 = send_over(sums)
    sums, held = chunk_sums(BLOCKS[1], BLOCKS[2], ids, hidden, down_weight, table, held, ids)
    over2 = send_over(sums)
    total3 = fold(features, spans(over3), sums[0])
    near2 = send_along(total3, 1)
    sums, held = chunk_sums(BLOCKS[2], BLOCKS[3], ids, hidden, down_weight, table, held, total3)
    late = features - features // 3 if pair else features
    over1 = send_over(sums, late)
    early = [send_along(part[:, late:], 1) for part in sums] if pair else []
    total2 = fold(features, spans(over2 + [near2]), sums[0])
    far0 = send_along(total2, 2)
    sums, _ = chunk_sums(BLOCKS[3], None, ids, hidden, down_weight, table, held, total2)
    if pair:
        sums = [fold(features, spans([part]) + [(got, 0, late, features - late)], total2) for part, got in zip(sums, early)]
    over0 = send_over(sums)
    near0 = send_along(fold(late, spans(over1, late), sums[0]), 1)
    rest = fold(features, spans([residual, far0]), ids, f32, LATE)
    rest = fold(features, spans([rest] + over0), ids, f32, LATE)
    return fold(features, spans([rest]) + spans([near0], late), ids)


def solution(mesh):
    return jax.shard_map(
        functools.partial(on_device, mesh.shape["expert"], mesh.shape["tp"]),
        mesh=mesh,
        in_specs=(
            P("expert", "dp", None, "tp"),
            P("expert", "tp", None),
            P(("dp", "expert"), None),
            P(("dp", "expert"), None),
            P(("dp", "expert"), "tp"),
        ),
        out_specs=P(("dp", "expert"), "tp"),
        check_vma=False,
    )
```

```python
import functools

import jax
import jax.numpy as jnp
from jax import lax
from jax.experimental import pallas as pl
from jax.experimental.pallas import tpu as pltpu
from jax.sharding import PartitionSpec as P

LANES = 128
TILE = 256
AHEAD = (2, 3, 3)
WINDOW = 6
CHUNKS = (((3, 0, 3),), ((2, 0, 3),), ((1, 0, 3),), ((0, 0, 3),))

LATE = 10**10

VMEM = pl.BlockSpec(memory_space=pltpu.VMEM)
SMEM = pl.BlockSpec(memory_space=pltpu.SMEM)
ANY = pl.BlockSpec(memory_space=pl.ANY)
HBM = pl.BlockSpec(memory_space=pltpu.HBM)
BF16 = jnp.bfloat16


class Strips:
    def __init__(self, ids_ref, weight_ref, chunk, expert, target, sem):
        self.rank, self.weight_ref, self.chunk = ids_ref[1], weight_ref.at[expert], chunk
        self.target, self.sem = target, sem

    def start(self):
        column = 0
        for block, start, stop, features in self.chunk:
            at = pl.multiple_of(lax.bitwise_xor(self.rank, block) * features + start, LANES)
            target = self.target.at[:, pl.ds(column, stop - start)]
            pltpu.make_async_copy(self.weight_ref.at[:, pl.ds(at, stop - start)], target, self.sem).start()
            column += stop - start

    def wait(self):
        pltpu.make_async_copy(self.weight_ref.at[:, pl.ds(0, self.target.shape[1])], self.target, self.sem).wait()


def columns_of(chunk):
    return sum(stop - start for _, start, stop, _ in chunk)


def balanced_dot(rows, weight_ref, finish):
    depth, width = weight_ref.shape
    even = width // TILE // 2 * 2 * TILE
    half = -(-depth // 2 // TILE) * TILE
    if width - even != TILE or half >= depth:
        even = width
    f32 = jnp.float32
    finish(0, even, jnp.dot(rows, weight_ref[:, :even], preferred_element_type=f32))
    if even < width:
        low = jnp.dot(rows[:, :half], weight_ref[:half, even:], preferred_element_type=f32)
        high = jnp.dot(rows[:, half:], weight_ref[half:, even:], preferred_element_type=f32)
        finish(even, width, low + high)


def product(rows_ref, weight_ref, partial, expert):
    sources, capacity, depth = rows_ref.shape

    def finish(start, stop, value):
        value = value.astype(partial.dtype)
        for source in range(sources):
            partial[source, expert * capacity : (expert + 1) * capacity, start:stop] = value[
                source * capacity : (source + 1) * capacity
            ]

    balanced_dot(rows_ref[...].reshape(sources * capacity, depth), weight_ref, finish)


def combine(ids_ref, table_refs, partial, outs, early_ref=None):
    mine = ids_ref[0]
    if len(outs) == 2:
        order = [(outs[0], table_refs[0], 1 - mine), (outs[1], table_refs[1], mine)]
    else:
        order = [(outs[0].at[s], table_refs[0].at[s], s) for s in range(partial.shape[0])]
    for i, (out_ref, table_ref, source) in enumerate(order):

        def finish(start, stop, value, i=i, out_ref=out_ref):
            tokens, room = out_ref.shape
            value = value.astype(out_ref.dtype)
            cut = min(stop, room)
            if start < cut:
                out_ref[:, start:cut] = value[:, : cut - start]
            if cut < stop:
                low = max(start, room)
                early_ref[i * tokens : (i + 1) * tokens, low - room : stop - room] = value[:, low - start :]

        balanced_dot(table_ref[...], partial.at[source], finish)


def share_table(ids_ref, routes, score, local, capacity):
    f32 = jnp.float32
    top, tokens = routes.shape
    width = local * capacity
    first = ids_ref[0] * local
    rows = lax.broadcasted_iota(jnp.int32, (tokens, tokens), 0)
    cols = lax.broadcasted_iota(jnp.int32, (tokens, tokens), 1)
    earlier = (rows < cols).astype(f32).astype(BF16)
    share = score / jnp.sum(score, axis=0, keepdims=True)
    experts = lax.broadcasted_iota(jnp.int32, (LANES // 8, tokens), 0)
    matches = [(experts == routes[k : k + 1]).astype(f32) for k in range(top)]
    onehot = functools.reduce(jnp.add, matches)
    before = jnp.dot(onehot.astype(BF16), earlier, preferred_element_type=f32)
    places = lax.broadcasted_iota(jnp.int32, (width, tokens), 0)
    entry = jnp.zeros((width, tokens), f32)
    for k in range(top):
        slot = jnp.sum(matches[k] * before, axis=0, keepdims=True).astype(jnp.int32)
        expert = routes[k : k + 1] - first
        at = jnp.where((expert >= 0) & (expert < local), expert * capacity + slot, -1)
        entry = jnp.where(places == at, share[k : k + 1], entry)
    return entry.T.astype(BF16)


class Stream:
    def __init__(self, groups):
        self.groups, self.begun, self.ended = groups, 0, 0
        for _ in range(WINDOW):
            self.begin()

    def begin(self):
        if self.begun < len(self.groups):
            for copy in self.groups[self.begun]:
                copy.start()
            self.begun += 1

    def end(self):
        for copy in self.groups[self.ended]:
            copy.wait()
        self.ended += 1
        self.begin()

    def finish(self):
        while self.ended < len(self.groups):
            self.end()


def first_kernel(chunk, ids_ref, hidden_ref, weight_ref, partial, stay_ref, weights, sems, hidden_sems):
    def bring(expert):
        copy = pltpu.make_async_copy(hidden_ref.at[expert], stay_ref.at[expert], hidden_sems.at[expert])
        return [copy, Strips(ids_ref, weight_ref, chunk, expert, weights.at[expert], sems.at[expert])]

    local = hidden_ref.shape[0]
    stream = Stream([bring(expert) for expert in range(local)])
    for expert in range(local):
        stream.end()
        product(stay_ref.at[expert], weights.at[expert], partial, expert)


def table_kernel(chunk, pair, capacity, *refs):
    refs = list(refs)
    ids_ref, partial, weight_ref = refs[:3]
    count = 2 if pair else 1
    routes_refs, score_refs, table_refs = refs[3 : 3 + count], refs[3 + count : 3 + 2 * count], refs[3 + 2 * count :]
    outs, (next_ref, next_sems) = table_refs[count:-2], table_refs[-2:]
    table_refs = table_refs[:count]
    local = table_refs[0].shape[-1] // capacity
    stream = Stream(
        [
            [Strips(ids_ref, weight_ref, chunk, expert, next_ref.at[expert], next_sems.at[expert])]
            for expert in range(next_ref.shape[0])
        ]
    )
    for routes_ref, score_ref, table_ref in zip(routes_refs, score_refs, table_refs):
        if pair:
            table_ref[...] = share_table(ids_ref, routes_ref[...], score_ref[...], local, capacity)
        else:
            for s in range(table_ref.shape[0]):
                table_ref[s] = share_table(ids_ref, routes_ref[s], score_ref[s], local, capacity)
    combine(ids_ref, table_refs, partial, outs)
    stream.finish()


def chunk_kernel(chunk, following, groups, early, ids_ref, hidden_ref, weight_ref, held_ref, *refs):
    refs = list(refs)
    table_refs = [refs.pop(0) for _ in range(groups)]
    del refs[0]
    outs = [refs.pop(0) for _ in range(groups)]
    early_ref = refs.pop(0) if early else None
    next_ref = refs.pop(0) if following else None
    weights, partial, sems, next_sems = refs
    local, ahead = hidden_ref.shape[0], held_ref.shape[0]

    own = [
        [Strips(ids_ref, weight_ref, chunk, e, weights.at[e - ahead], sems.at[e - ahead])]
        for e in range(ahead, local)
    ]
    later = [
        [Strips(ids_ref, weight_ref, following, e, next_ref.at[e], next_sems.at[e])]
        for e in range(next_ref.shape[0] if following else 0)
    ]
    stream = Stream(own + later)
    for expert in range(local):
        if expert >= ahead:
            stream.end()
            product(hidden_ref.at[expert], weights.at[expert - ahead], partial, expert)
        else:
            product(hidden_ref.at[expert], held_ref.at[expert], partial, expert)
    combine(ids_ref, table_refs, partial, outs, early_ref)
    stream.finish()


def fold_kernel(spans, *refs):
    *terms, _, sum_ref = refs
    tokens = sum_ref.shape[0]
    edges = sorted({edge for _, _, at, width in spans for edge in (at, at + width)})
    for low, high in zip(edges[:-1], edges[1:]):
        parts = [
            term[row : row + tokens, source + low - at : source + high - at].astype(jnp.float32)
            for term, (row, source, at, width) in zip(terms, spans)
            if at <= low < at + width
        ]
        sum_ref[:, low:high] = functools.reduce(jnp.add, parts).astype(sum_ref.dtype)


def shape(*dims):
    return jax.ShapeDtypeStruct(dims, BF16)


def cost(flops, count):
    return pl.CostEstimate(flops=flops, bytes_accessed=2 * count, transcendentals=0)


COST = cost(1000, 1000)


def first_products(chunk, ids, hidden, weight):
    local, sources, capacity, depth = hidden.shape
    columns = columns_of(chunk)
    return pl.pallas_call(
        functools.partial(first_kernel, chunk),
        in_specs=[SMEM, HBM, HBM],
        out_specs=[VMEM] * 2,
        out_shape=[shape(sources, local * capacity, columns), shape(*hidden.shape)],
        scratch_shapes=[
            pltpu.VMEM((local, depth, columns), BF16),
            pltpu.SemaphoreType.DMA((local,)),
            pltpu.SemaphoreType.DMA((local,)),
        ],
        cost_estimate=cost(2 * sources * local * capacity * columns * depth, local * depth * columns),
        compiler_params=pltpu.CompilerParams(vmem_limit_bytes=46 << 20),
        name="first",
    )(ids, hidden, weight)


def group_shapes(pair, sources, tokens, width):
    return [shape(tokens, width)] * 2 if pair else [shape(sources, tokens, width)]


def tables(following, ids, partial, weight, routes, scores, capacity):
    sources, width, columns = partial.shape
    pair = len(routes) == 2
    tokens = routes[0].shape[-1]
    depth = weight.shape[1]
    ahead = min(AHEAD[0], width // capacity)
    table = [shape(tokens, width)] * 2 if pair else [shape(sources, tokens, width)]
    outs = group_shapes(pair, sources, tokens, columns)
    results = pl.pallas_call(
        functools.partial(table_kernel, following, pair, capacity),
        in_specs=[SMEM, VMEM, HBM] + [VMEM] * (2 * len(routes)),
        out_specs=[VMEM] * (len(table) + len(outs) + 1),
        out_shape=table + outs + [shape(ahead, depth, columns_of(following))],
        scratch_shapes=[pltpu.SemaphoreType.DMA((ahead,))],
        cost_estimate=COST,
        compiler_params=pltpu.CompilerParams(vmem_limit_bytes=12 << 20),
        name="tables",
    )(ids, partial, weight, *routes, *scores)
    return results[: len(table)], results[len(table) : -1], results[-1]


def chunk_sums(chunk, following, ahead_next, early, ids, hidden, weight, table, held, after):
    local, sources, capacity, depth = hidden.shape
    tokens = table[0].shape[-2]
    ahead, _, columns = held.shape
    brought = max(local - ahead, 1)
    groups = len(table)
    outs = group_shapes(groups == 2, sources, tokens, columns - early)
    if early:
        outs.append(shape(groups * tokens, early))
    if following:
        outs.append(shape(min(ahead_next, local), depth, columns_of(following)))
    flops = 2 * sources * local * capacity * columns * (depth + tokens)
    results = pl.pallas_call(
        functools.partial(chunk_kernel, chunk, following, groups, early),
        in_specs=[SMEM, VMEM, HBM, VMEM] + [VMEM] * groups + [ANY],
        out_specs=[VMEM] * len(outs),
        out_shape=outs,
        scratch_shapes=[
            pltpu.VMEM((brought, depth, columns), BF16),
            pltpu.VMEM((sources, local * capacity, columns), BF16),
            pltpu.SemaphoreType.DMA((brought,)),
            pltpu.SemaphoreType.DMA((local,)),
        ],
        cost_estimate=cost(flops, local * depth * columns) if following else COST,
        compiler_params=pltpu.CompilerParams(vmem_limit_bytes=20 << 20),
        name="chunk",
    )(ids, hidden, weight, held, *table, after)
    results = list(results)
    return results[:groups], results[groups] if early else None, results[-1] if following else None


def fold(tokens, width, terms, after, dtype=BF16, flops=1000):
    arrays, spans = [term[0] for term in terms], [term[1:] for term in terms]
    return pl.pallas_call(
        functools.partial(fold_kernel, spans),
        in_specs=[VMEM] * len(terms) + [ANY],
        out_specs=VMEM,
        out_shape=jax.ShapeDtypeStruct((tokens, width), dtype),
        cost_estimate=cost(flops, 1000),
        compiler_params=pltpu.CompilerParams(vmem_limit_bytes=6 << 20),
        name="fold",
    )(*arrays, after)


def on_device(experts, ranks, hidden, down_weight, routes, route_weight, residual):
    f32 = jnp.float32
    capacity = hidden.shape[2]
    tokens, features = residual.shape
    pair = experts == 2
    ids = jnp.stack([lax.axis_index("expert"), lax.axis_index("tp")]).astype(jnp.int32)
    routes, scores = routes.T, route_weight.T
    swap = [(0, 1), (1, 0)]
    if pair:
        routes, scores = [lax.ppermute(routes, "expert", swap), routes], [lax.ppermute(scores, "expert", swap), scores]
    else:
        routes, scores = [lax.all_gather(routes, "expert")], [lax.all_gather(scores, "expert")]

    third = features // 3
    chunks = [
        tuple((block, start * third, stop * third, features) for block, start, stop in chunk) for chunk in CHUNKS
    ]

    def send_over(sums):
        if pair:
            return [sums[1], lax.ppermute(sums[0], "expert", swap)]
        return [lax.psum_scatter(sums[0], "expert", scatter_dimension=0, tiled=True).reshape(tokens, -1)]

    def send_along(total, flip):
        return lax.ppermute(total, "tp", [(r, r ^ flip) for r in range(ranks)])

    def spans(arrays, source=0, at=0, width=features, row=0):
        return [(array, row, source, at, width) for array in arrays]

    def total(width, terms, after, dtype=BF16, flops=1000):
        return fold(tokens, width, terms, after, dtype, flops)

    partial, hidden = first_products(chunks[0], ids, hidden, down_weight)
    table, sums, held = tables(chunks[1], ids, partial, down_weight, routes, scores, capacity)
    over3 = send_over(sums)
    sums, _, held = chunk_sums(chunks[1], chunks[2], AHEAD[1], 0, ids, hidden, down_weight, table, held, ids)
    over2 = send_over(sums)
    total3 = total(features, spans(over3), sums[0])
    near2 = send_along(total3, 1)
    early = third if pair else 0
    sums, part, held = chunk_sums(chunks[2], chunks[3], AHEAD[2], early, ids, hidden, down_weight, table, held, total3)
    over1 = send_over(sums)
    parts = [send_along(part[at : at + tokens], 1) for at in (0, tokens)] if pair else []
    total2 = total(features, spans(over2 + [near2]), sums[0])
    far0 = send_along(total2, 2)
    sums, _, _ = chunk_sums(chunks[3], None, 0, 0, ids, hidden, down_weight, table, held, total2)
    kept = features - early
    if pair:
        over0 = spans([sums[1], lax.ppermute(sums[0][:, :kept], "expert", swap)], width=kept)
        late = total(early, spans(sums[:1], kept, 0, early) + spans(parts[:1], width=early), ids)
        ends = spans([sums[1]], kept, kept, early) + spans([lax.ppermute(late, "expert", swap), parts[1]], 0, kept, early)
    else:
        over0, ends = spans(send_over(sums)), []
    near0 = send_along(total(kept, spans(over1, width=kept), sums[0]), 1)
    rest = total(features, spans([residual, far0]), ids, f32, LATE)
    for terms in (over0, ends):
        rest = total(features, spans([rest]) + terms, ids, f32, LATE) if terms else rest
    return total(features, spans([rest]) + spans([near0], width=kept), ids)


def solution(mesh):
    return jax.shard_map(
        functools.partial(on_device, mesh.shape["expert"], mesh.shape["tp"]),
        mesh=mesh,
        in_specs=(
            P("expert", "dp", None, "tp"),
            P("expert", "tp", None),
            P(("dp", "expert"), None),
            P(("dp", "expert"), None),
            P(("dp", "expert"), "tp"),
        ),
        out_specs=P(("dp", "expert"), "tp"),
        check_vma=False,
    )
```

```python
import functools

import jax
import jax.numpy as jnp
from jax import lax
from jax.experimental import pallas as pl
from jax.experimental.pallas import tpu as pltpu
from jax.sharding import PartitionSpec as P

LANES = 128
TILE = 256
AHEAD = (2, 3, 3)
WINDOW = 6
CHUNKS = (((3, 0, 3),), ((2, 0, 3),), ((1, 0, 3),), ((0, 0, 3),))

LATE = 10**10

VMEM = pl.BlockSpec(memory_space=pltpu.VMEM)
SMEM = pl.BlockSpec(memory_space=pltpu.SMEM)
ANY = pl.BlockSpec(memory_space=pl.ANY)
HBM = pl.BlockSpec(memory_space=pltpu.HBM)
BF16 = jnp.bfloat16


class Strips:
    def __init__(self, ids_ref, weight_ref, chunk, expert, target, sem):
        self.rank, self.weight_ref, self.chunk = ids_ref[1], weight_ref.at[expert], chunk
        self.target, self.sem = target, sem

    def start(self):
        column = 0
        for block, start, stop, features in self.chunk:
            at = pl.multiple_of(lax.bitwise_xor(self.rank, block) * features + start, LANES)
            target = self.target.at[:, pl.ds(column, stop - start)]
            pltpu.make_async_copy(self.weight_ref.at[:, pl.ds(at, stop - start)], target, self.sem).start()
            column += stop - start

    def wait(self):
        pltpu.make_async_copy(self.weight_ref.at[:, pl.ds(0, self.target.shape[1])], self.target, self.sem).wait()


def columns_of(chunk):
    return sum(stop - start for _, start, stop, _ in chunk)


def balanced_dot(rows, weight_ref, finish):
    depth, width = weight_ref.shape
    even = width // TILE // 2 * 2 * TILE
    half = -(-depth // 2 // TILE) * TILE
    if width - even != TILE or half >= depth:
        even = width
    f32 = jnp.float32
    finish(0, even, jnp.dot(rows, weight_ref[:, :even], preferred_element_type=f32))
    if even < width:
        low = jnp.dot(rows[:, :half], weight_ref[:half, even:], preferred_element_type=f32)
        high = jnp.dot(rows[:, half:], weight_ref[half:, even:], preferred_element_type=f32)
        finish(even, width, low + high)


def product(rows_ref, weight_ref, partial, expert):
    sources, capacity, depth = rows_ref.shape

    def finish(start, stop, value):
        value = value.astype(partial.dtype)
        for source in range(sources):
            partial[source, expert * capacity : (expert + 1) * capacity, start:stop] = value[
                source * capacity : (source + 1) * capacity
            ]

    balanced_dot(rows_ref[...].reshape(sources * capacity, depth), weight_ref, finish)


def combine(ids_ref, table_refs, partial, outs, early_ref=None):
    mine = ids_ref[0]
    if len(outs) == 2:
        order = [(outs[0], table_refs[0], 1 - mine), (outs[1], table_refs[1], mine)]
    else:
        order = [(outs[0].at[s], table_refs[0].at[s], s) for s in range(partial.shape[0])]
    for i, (out_ref, table_ref, source) in enumerate(order):

        def finish(start, stop, value, i=i, out_ref=out_ref):
            tokens, room = out_ref.shape
            value = value.astype(out_ref.dtype)
            cut = min(stop, room)
            if start < cut:
                out_ref[:, start:cut] = value[:, : cut - start]
            if cut < stop:
                low = max(start, room)
                early_ref[i * tokens : (i + 1) * tokens, low - room : stop - room] = value[:, low - start :]

        balanced_dot(table_ref[...], partial.at[source], finish)


def share_table(ids_ref, routes, score, local, capacity):
    f32 = jnp.float32
    top, tokens = routes.shape
    width = local * capacity
    first = ids_ref[0] * local
    rows = lax.broadcasted_iota(jnp.int32, (tokens, tokens), 0)
    cols = lax.broadcasted_iota(jnp.int32, (tokens, tokens), 1)
    earlier = (rows < cols).astype(f32).astype(BF16)
    share = score / jnp.sum(score, axis=0, keepdims=True)
    experts = lax.broadcasted_iota(jnp.int32, (LANES // 8, tokens), 0)
    matches = [(experts == routes[k : k + 1]).astype(f32) for k in range(top)]
    onehot = functools.reduce(jnp.add, matches)
    before = jnp.dot(onehot.astype(BF16), earlier, preferred_element_type=f32)
    places = lax.broadcasted_iota(jnp.int32, (width, tokens), 0)
    entry = jnp.zeros((width, tokens), f32)
    for k in range(top):
        slot = jnp.sum(matches[k] * before, axis=0, keepdims=True).astype(jnp.int32)
        expert = routes[k : k + 1] - first
        at = jnp.where((expert >= 0) & (expert < local), expert * capacity + slot, -1)
        entry = jnp.where(places == at, share[k : k + 1], entry)
    return entry.T.astype(BF16)


class Stream:
    def __init__(self, groups):
        self.groups, self.begun, self.ended = groups, 0, 0
        for _ in range(WINDOW):
            self.begin()

    def begin(self):
        if self.begun < len(self.groups):
            for copy in self.groups[self.begun]:
                copy.start()
            self.begun += 1

    def end(self):
        for copy in self.groups[self.ended]:
            copy.wait()
        self.ended += 1
        self.begin()

    def finish(self):
        while self.ended < len(self.groups):
            self.end()


def first_kernel(chunk, ids_ref, hidden_ref, weight_ref, partial, stay_ref, weights, sems, hidden_sems):
    def bring(expert):
        copy = pltpu.make_async_copy(hidden_ref.at[expert], stay_ref.at[expert], hidden_sems.at[expert])
        return [copy, Strips(ids_ref, weight_ref, chunk, expert, weights.at[expert], sems.at[expert])]

    local = hidden_ref.shape[0]
    stream = Stream([bring(expert) for expert in range(local)])
    for expert in range(local):
        stream.end()
        product(stay_ref.at[expert], weights.at[expert], partial, expert)


def table_kernel(chunk, pair, capacity, *refs):
    refs = list(refs)
    ids_ref, partial, weight_ref = refs[:3]
    count = 2 if pair else 1
    routes_refs, score_refs, table_refs = refs[3 : 3 + count], refs[3 + count : 3 + 2 * count], refs[3 + 2 * count :]
    outs, (next_ref, next_sems) = table_refs[count:-2], table_refs[-2:]
    table_refs = table_refs[:count]
    local = table_refs[0].shape[-1] // capacity
    stream = Stream(
        [
            [Strips(ids_ref, weight_ref, chunk, expert, next_ref.at[expert], next_sems.at[expert])]
            for expert in range(next_ref.shape[0])
        ]
    )
    for routes_ref, score_ref, table_ref in zip(routes_refs, score_refs, table_refs):
        if pair:
            table_ref[...] = share_table(ids_ref, routes_ref[...], score_ref[...], local, capacity)
        else:
            for s in range(table_ref.shape[0]):
                table_ref[s] = share_table(ids_ref, routes_ref[s], score_ref[s], local, capacity)
    combine(ids_ref, table_refs, partial, outs)
    stream.finish()


def chunk_kernel(chunk, following, groups, early, ids_ref, hidden_ref, weight_ref, held_ref, *refs):
    refs = list(refs)
    table_refs = [refs.pop(0) for _ in range(groups)]
    del refs[0]
    outs = [refs.pop(0) for _ in range(groups)]
    early_ref = refs.pop(0) if early else None
    next_ref = refs.pop(0) if following else None
    weights, partial, sems, next_sems = refs
    local, ahead = hidden_ref.shape[0], held_ref.shape[0]

    own = [
        [Strips(ids_ref, weight_ref, chunk, e, weights.at[e - ahead], sems.at[e - ahead])]
        for e in range(ahead, local)
    ]
    later = [
        [Strips(ids_ref, weight_ref, following, e, next_ref.at[e], next_sems.at[e])]
        for e in range(next_ref.shape[0] if following else 0)
    ]
    stream = Stream(own + later)
    for expert in range(local):
        if expert >= ahead:
            stream.end()
            product(hidden_ref.at[expert], weights.at[expert - ahead], partial, expert)
        else:
            product(hidden_ref.at[expert], held_ref.at[expert], partial, expert)
    combine(ids_ref, table_refs, partial, outs, early_ref)
    stream.finish()


def fold_kernel(spans, *refs):
    *terms, _, sum_ref = refs
    tokens = sum_ref.shape[0]
    edges = sorted({edge for _, _, at, width in spans for edge in (at, at + width)})
    for low, high in zip(edges[:-1], edges[1:]):
        parts = [
            term[row : row + tokens, source + low - at : source + high - at].astype(jnp.float32)
            for term, (row, source, at, width) in zip(terms, spans)
            if at <= low < at + width
        ]
        sum_ref[:, low:high] = functools.reduce(jnp.add, parts).astype(sum_ref.dtype)


def shape(*dims):
    return jax.ShapeDtypeStruct(dims, BF16)


def cost(flops, count):
    return pl.CostEstimate(flops=flops, bytes_accessed=2 * count, transcendentals=0)


COST = cost(1000, 1000)


def first_products(chunk, ids, hidden, weight):
    local, sources, capacity, depth = hidden.shape
    columns = columns_of(chunk)
    return pl.pallas_call(
        functools.partial(first_kernel, chunk),
        in_specs=[SMEM, HBM, HBM],
        out_specs=[VMEM] * 2,
        out_shape=[shape(sources, local * capacity, columns), shape(*hidden.shape)],
        scratch_shapes=[
            pltpu.VMEM((local, depth, columns), BF16),
            pltpu.SemaphoreType.DMA((local,)),
            pltpu.SemaphoreType.DMA((local,)),
        ],
        cost_estimate=cost(2 * sources * local * capacity * columns * depth, local * depth * columns),
        compiler_params=pltpu.CompilerParams(vmem_limit_bytes=46 << 20),
        name="first",
    )(ids, hidden, weight)


def group_shapes(pair, sources, tokens, width):
    return [shape(tokens, width)] * 2 if pair else [shape(sources, tokens, width)]


def tables(following, ids, partial, weight, routes, scores, capacity):
    sources, width, columns = partial.shape
    pair = len(routes) == 2
    tokens = routes[0].shape[-1]
    depth = weight.shape[1]
    ahead = min(AHEAD[0], width // capacity)
    table = [shape(tokens, width)] * 2 if pair else [shape(sources, tokens, width)]
    outs = group_shapes(pair, sources, tokens, columns)
    results = pl.pallas_call(
        functools.partial(table_kernel, following, pair, capacity),
        in_specs=[SMEM, VMEM, HBM] + [VMEM] * (2 * len(routes)),
        out_specs=[VMEM] * (len(table) + len(outs) + 1),
        out_shape=table + outs + [shape(ahead, depth, columns_of(following))],
        scratch_shapes=[pltpu.SemaphoreType.DMA((ahead,))],
        cost_estimate=COST,
        compiler_params=pltpu.CompilerParams(vmem_limit_bytes=12 << 20),
        name="tables",
    )(ids, partial, weight, *routes, *scores)
    return results[: len(table)], results[len(table) : -1], results[-1]


def chunk_sums(chunk, following, ahead_next, early, ids, hidden, weight, table, held, after):
    local, sources, capacity, depth = hidden.shape
    tokens = table[0].shape[-2]
    ahead, _, columns = held.shape
    brought = max(local - ahead, 1)
    groups = len(table)
    outs = group_shapes(groups == 2, sources, tokens, columns - early)
    if early:
        outs.append(shape(groups * tokens, early))
    if following:
        outs.append(shape(min(ahead_next, local), depth, columns_of(following)))
    flops = 2 * sources * local * capacity * columns * (depth + tokens)
    results = pl.pallas_call(
        functools.partial(chunk_kernel, chunk, following, groups, early),
        in_specs=[SMEM, VMEM, HBM, VMEM] + [VMEM] * groups + [ANY],
        out_specs=[VMEM] * len(outs),
        out_shape=outs,
        scratch_shapes=[
            pltpu.VMEM((brought, depth, columns), BF16),
            pltpu.VMEM((sources, local * capacity, columns), BF16),
            pltpu.SemaphoreType.DMA((brought,)),
            pltpu.SemaphoreType.DMA((local,)),
        ],
        cost_estimate=cost(flops, local * depth * columns) if following else COST,
        compiler_params=pltpu.CompilerParams(vmem_limit_bytes=20 << 20),
        name="chunk",
    )(ids, hidden, weight, held, *table, after)
    results = list(results)
    return results[:groups], results[groups] if early else None, results[-1] if following else None


def fold(tokens, width, terms, after, dtype=BF16, flops=1000):
    arrays, spans = [term[0] for term in terms], [term[1:] for term in terms]
    return pl.pallas_call(
        functools.partial(fold_kernel, spans),
        in_specs=[VMEM] * len(terms) + [ANY],
        out_specs=VMEM,
        out_shape=jax.ShapeDtypeStruct((tokens, width), dtype),
        cost_estimate=cost(flops, 1000),
        compiler_params=pltpu.CompilerParams(vmem_limit_bytes=6 << 20),
        name="fold",
    )(*arrays, after)


def on_device(experts, ranks, hidden, down_weight, routes, route_weight, residual):
    f32 = jnp.float32
    capacity = hidden.shape[2]
    tokens, features = residual.shape
    pair = experts == 2
    ids = jnp.stack([lax.axis_index("expert"), lax.axis_index("tp")]).astype(jnp.int32)
    routes, scores = routes.T, route_weight.T
    swap = [(0, 1), (1, 0)]
    if pair:
        routes, scores = [lax.ppermute(routes, "expert", swap), routes], [lax.ppermute(scores, "expert", swap), scores]
    else:
        routes, scores = [lax.all_gather(routes, "expert")], [lax.all_gather(scores, "expert")]

    third = features // 3
    chunks = [
        tuple((block, start * third, stop * third, features) for block, start, stop in chunk) for chunk in CHUNKS
    ]

    def send_over(sums):
        if pair:
            return [sums[1], lax.ppermute(sums[0], "expert", swap)]
        return [lax.psum_scatter(sums[0], "expert", scatter_dimension=0, tiled=True).reshape(tokens, -1)]

    def send_along(total, flip):
        return lax.ppermute(total, "tp", [(r, r ^ flip) for r in range(ranks)])

    def spans(arrays, source=0, at=0, width=features, row=0):
        return [(array, row, source, at, width) for array in arrays]

    def total(width, terms, after, dtype=BF16, flops=1000):
        return fold(tokens, width, terms, after, dtype, flops)

    partial, hidden = first_products(chunks[0], ids, hidden, down_weight)
    table, sums, held = tables(chunks[1], ids, partial, down_weight, routes, scores, capacity)
    over3 = send_over(sums)
    sums, _, held = chunk_sums(chunks[1], chunks[2], AHEAD[1], 0, ids, hidden, down_weight, table, held, ids)
    over2 = send_over(sums)
    total3 = total(features, spans(over3), sums[0])
    near2 = send_along(total3, 1)
    early = third if pair else 0
    sums, part, held = chunk_sums(chunks[2], chunks[3], AHEAD[2], early, ids, hidden, down_weight, table, held, total3)
    over1 = send_over(sums)
    parts = [send_along(part[at : at + tokens], 1) for at in (0, tokens)] if pair else []
    total2 = total(features, spans(over2 + [near2]), sums[0])
    far0 = send_along(total2, 2)
    sums, _, _ = chunk_sums(chunks[3], None, 0, 0, ids, hidden, down_weight, table, held, total2)
    kept = features - early
    if pair:
        late = total(features, spans(sums[:1]) + spans(parts[:1], 0, kept, early), ids)
        over0 = spans([sums[1], lax.ppermute(late, "expert", swap)])
        ends = spans([parts[1]], 0, kept, early)
    else:
        over0, ends = spans(send_over(sums)), []
    near0 = send_along(total(kept, spans(over1, width=kept), sums[0]), 1)
    rest = total(features, spans([residual, far0]), ids, f32, LATE)
    for terms in (over0, ends):
        rest = total(features, spans([rest]) + terms, ids, f32, LATE) if terms else rest
    return total(features, spans([rest]) + spans([near0], width=kept), ids)


def solution(mesh):
    return jax.shard_map(
        functools.partial(on_device, mesh.shape["expert"], mesh.shape["tp"]),
        mesh=mesh,
        in_specs=(
            P("expert", "dp", None, "tp"),
            P("expert", "tp", None),
            P(("dp", "expert"), None),
            P(("dp", "expert"), None),
            P(("dp", "expert"), "tp"),
        ),
        out_specs=P(("dp", "expert"), "tp"),
        check_vma=False,
    )
```
